32 devices in a mesh: grp: 2 (over y), gz: 4 (over z), phi: 4 (over x, core).
Axes of the slice: x: 2, y: 2, z: 4, core: 2. Of those that a mesh axis runs over, the one named last changes fastest.
Arguments:
- charge: bfloat16 [2048, 128, 256], P(('grp', 'phi'), 'gz'), parts along dimension 0, may hold values from -44 to 44
- orders: int32 [64], replicated, may hold values from 1 to 255, as said below
- electrode: int32 [128, 256], P('gz'), may hold values 0 or 1
Outputs:
- distortion: bfloat16 [2048, 128, 256], P(('grp', 'phi'), 'gz'), parts along dimension 0
- potential: float32 [256, 128, 256], P(('grp', 'phi'), 'gz'), parts along dimension 0
The draws below stay inside these ranges and needn't reach their ends.
There are 2 independent parts, one for each index of `grp`. The reference program is written for one: setup_inputs(seed, part) draws one part's arguments, and reference() takes and returns one part's arrays. A program takes and returns all parts, laid end to end along the dimension named above; an argument that names none is the same for every part. Nothing has to cross between parts.
Inputs may be any that keep to these rules, and one draw needn't show every extreme that they name: The 64 orders are distinct, and 1 and 255 are among them.
All inputs are finite; a program needn't handle non-finite values. No bound on the sum of `electrode` on one device may be relied on, other than what follows from the above.
Results may differ from the reference program's by a relative error of at most 0.0059.
Values may be sent and summed in bfloat16 or wider, within the bound.
A program may use at most 64 MiB of HBM per device.

```python
import math
import jax
import jax.numpy as jnp
from jax import lax

PHI = 1024
ORDERS = 64
MODES = 128
NR = 256
SWEEPS = 4
NZ = 128
N_PHI = 4


def draw_charge(key, part):
    layers = jax.random.truncated_normal(key, -4.0, 4.0, (PHI, NZ + 1, NR), jnp.float32)
    layers = 6.0 * layers
    return (layers[:, 1:] - 0.8 * layers[:, :-1]).astype(jnp.bfloat16)


def draw_orders(key, part):
    first_key, second_key = jax.random.split(jax.random.fold_in(key, 7))
    limit = PHI // 4
    middle = jax.random.permutation(first_key, limit - 3).astype(jnp.int32) + 2
    ends = jnp.array([1, limit - 1], dtype=jnp.int32)
    values = jnp.concatenate([ends, middle[:ORDERS - 2]], 0)
    placing = jax.random.permutation(second_key, ORDERS).astype(jnp.int32)
    return jnp.take(values, placing, axis=0)


def place_ends(values, stream_key, smallest, top_value):
    shape = values.shape
    index_at = [jax.random.randint(jax.random.fold_in(stream_key, axis), (), 0, shape[axis]) for axis in range(len(shape))]
    values = values.at[tuple(index_at)].set(smallest)
    longest = shape.index(max(shape))
    index_at[longest] = (index_at[longest] + 1) % shape[longest]
    return values.at[tuple(index_at)].set(top_value)


def setup_inputs(seed: int = 0, part: int = 0) -> dict:
    key_list = jax.random.split(jax.random.key(seed), 4)
    part_keys = jax.random.split(jax.random.fold_in(key_list[3], part), 4)
    charge = draw_charge(jax.random.fold_in(jax.random.fold_in(key_list[3], part), 71), part)
    orders = draw_orders(jax.random.fold_in(key_list[3], 71), part)
    electrode = place_ends((jax.random.randint(key_list[2], (NZ, NR), 0, 16) < 1).astype(jnp.int32), jax.random.fold_in(key_list[2], 1), 0, 1)
    return dict(charge=charge, orders=orders, electrode=electrode)


def make_table(orders):
    positions = jnp.arange(PHI, dtype=jnp.int32)
    phase_int = (orders[:, None] * positions[None, :]) % PHI
    angles = phase_int.astype(jnp.float32) * (2.0 * math.pi / PHI)
    return jnp.concatenate([jnp.cos(angles), jnp.sin(angles)], 0).astype(jnp.bfloat16)


def radial_terms(order_values, radial_cells):
    radius = jnp.arange(radial_cells, dtype=jnp.float32) + (radial_cells // 2 + 0.5)
    outer_coef = 1.0 + 0.5 / radius
    inner_coef = 1.0 - 0.5 / radius
    diagonal = 4.0 + (order_values[:, None] / radius[None, :]) ** 2
    return outer_coef, inner_coef, diagonal[:, None, :]


def radial_sum(field_now, outer_coef, inner_coef):
    zero_plane = jnp.zeros_like(field_now[..., :1])
    upper_cell = jnp.concatenate([field_now[..., 1:], zero_plane], -1)
    lower_cell = jnp.concatenate([zero_plane, field_now[..., :-1]], -1)
    return outer_coef * upper_cell + inner_coef * lower_cell, upper_cell, lower_cell


def reference(charge, orders, electrode):
    basis_table = make_table(orders)
    flattened = charge.reshape(PHI, NZ * NR)
    source = jnp.dot(basis_table, flattened, preferred_element_type=jnp.float32).reshape(MODES, NZ, NR) * PHI ** -0.5
    order_values = jnp.concatenate([orders, orders]).astype(jnp.float32)
    outer_coef, inner_coef, diagonal = radial_terms(order_values, NR)
    open_cells = (1 - electrode).astype(jnp.float32)
    potential = open_cells * source / diagonal
    for sweep in range(SWEEPS):
        zero_plane = jnp.zeros_like(potential[:, :1])
        upper_plane = jnp.concatenate([potential[:, 1:], zero_plane], 1)
        lower_plane = jnp.concatenate([zero_plane, potential[:, :-1]], 1)
        radial, _, _ = radial_sum(potential, outer_coef, inner_coef)
        neighbours = upper_plane + lower_plane + radial
        potential = open_cells * (source + neighbours) / diagonal
    _, upper_cell, lower_cell = radial_sum(potential, outer_coef, inner_coef)
    radial_field = 0.5 * (upper_cell - lower_cell)
    suffix = lax.cumsum(radial_field, axis=1, reverse=True)
    mode_shift = (suffix * NZ ** -0.5).astype(jnp.bfloat16).reshape(MODES, NZ * NR)
    blocks = basis_table.T.reshape(N_PHI, PHI // N_PHI, MODES)

    def synthesize(weights):
        return (jnp.dot(weights, mode_shift, preferred_element_type=jnp.float32) * MODES ** -0.5).astype(jnp.bfloat16)

    distortion = lax.map(synthesize, blocks).reshape(PHI, NZ, NR)
    return distortion, potential
```

```python
import functools
import math

import jax
import jax.numpy as jnp
from jax import lax
from jax.experimental import pallas as pl
from jax.experimental.pallas import tpu as pltpu
from jax.sharding import PartitionSpec as P

PHI = 1024
ORDERS = 64
MODES = 128
SWEEPS = 4
MESH = pl.DeviceIdType.MESH


def kernel(
    n, ngz, chunks, groups,
    basis_ref, ch_ref, open_ref, inv_ref, coef_ref,
    pot_ref, ms_ref,
    send1, keep, recv1, l2send, l2recv, openx, srcx, pa, pb, loc, tot, trecv,
    l1_s, l1_r, l2_s, l2_r, op_s, op_r, ha_s, ha_r, to_s, to_r, ag_s, ag_r, sb_s, sb_r, fw_s, fw_r,
):
    nq = n // 2
    depth, _, cells = ch_ref.shape
    rows = inv_ref.shape[1]
    mode_rows = chunks * rows
    zg = depth // groups
    h = SWEEPS
    me = lax.axis_index("phi")
    gz = lax.axis_index("gz")
    p, core = me // 2, lax.rem(me, 2)
    sib = p * 2 + 1 - core

    def remote(src, dst, s, r, where):
        return pltpu.make_async_remote_copy(
            src_ref=src, dst_ref=dst, send_sem=s, recv_sem=r, device_id=where, device_id_type=MESH
        )

    def quad(d):
        return lax.rem(p + d, nq)

    def slab(d):
        return lax.rem(gz + d, ngz)

    barrier = pltpu.get_barrier_semaphore()
    pl.semaphore_signal(barrier, inc=1, device_id={"phi": sib}, device_id_type=MESH)
    for d in range(1, nq):
        pl.semaphore_signal(
            barrier, inc=1, device_id={"phi": quad(d) * 2 + core}, device_id_type=MESH
        )
    for d in range(1, ngz):
        pl.semaphore_signal(barrier, inc=1, device_id={"gz": slab(d)}, device_id_type=MESH)

    def l1(c, g):
        part = (c, slice(None), pl.ds(g * zg, zg))
        return remote(send1.at[part], recv1.at[part], l1_s.at[c, g], l1_r.at[c, g], {"phi": sib})

    def l2(c, g, d):
        part = (c, d - 1, pl.ds(g * zg, zg))
        return remote(
            l2send.at[part], l2recv.at[part], l2_s.at[c, g, d - 1], l2_r.at[c, g, d - 1],
            {"phi": quad(d) * 2 + core},
        )

    def both_ways(action):
        @pl.when(gz > 0)
        def _():
            action(0, gz - 1)

        @pl.when(gz < ngz - 1)
        def _():
            action(1, gz + 1)

    def halo(buf_src, first, buf_dst, s, r, way, where):
        src = pl.ds(first, h) if way == 0 else pl.ds(first + depth - h, h)
        dst = pl.ds(h + depth, h) if way == 0 else pl.ds(0, h)
        return remote(buf_src.at[src], buf_dst.at[dst], s.at[way], r.at[way], {"gz": where})

    def halo_send(*args):
        both_ways(lambda way, where: halo(*args, way, where).start())

    def halo_wait_send(*args):
        both_ways(lambda way, where: halo(*args, way, where).wait_send())

    def halo_wait_recv(*args):
        both_ways(lambda way, where: halo(*args, 1 - way, where).wait_recv())

    def total(c, d):
        return remote(
            tot.at[c], trecv.at[c, d - 1], to_s.at[c, d - 1], to_r.at[c, d - 1], {"gz": slab(d)}
        )

    def block(owner, c):
        start = pl.multiple_of(owner * mode_rows + c * rows, rows)
        return ms_ref.at[:, pl.ds(start, rows), :]

    def gather(c, d):
        b = block(me, c)
        return remote(b, b, ag_s.at[c, d - 1], ag_r.at[c, d - 1], {"phi": quad(d) * 2 + core})

    def gather_sib(c):
        b = block(me, c)
        return remote(b, b, sb_s.at[c], sb_r.at[c], {"phi": sib})

    def forward(c, d):
        b = block(lax.rem(p - d + nq, nq) * 2 + core, c)
        return remote(b, b, fw_s.at[c, d - 1], fw_r.at[c, d - 1], {"phi": sib})

    openx[pl.ds(h, depth)] = open_ref[...]
    edge = jnp.zeros((h,) + srcx.shape[2:], jnp.float32)

    def no_slab(first):
        openx[pl.ds(first, h)] = jnp.zeros((h,) + openx.shape[1:], jnp.float32)
        for c in range(chunks):
            srcx[c, pl.ds(first, h)] = edge

    @pl.when(gz == 0)
    def _():
        no_slab(0)

    @pl.when(gz == ngz - 1)
    def _():
        no_slab(h + depth)

    pl.semaphore_wait(barrier, nq + ngz - 1)
    open_args = (open_ref, 0, openx, op_s, op_r)
    halo_send(*open_args)

    for g in range(groups):
        def plane(i, _, g=g):
            z = g * zg + i
            full = jnp.dot(basis_ref[...], ch_ref[z], preferred_element_type=jnp.float32)
            at = 0
            for buf in (send1, keep):
                for c in range(chunks):
                    for q in range(nq):
                        buf[c, q, z] = full[at : at + rows]
                        at += rows
            return 0

        lax.fori_loop(0, zg, plane, 0)
        for c in range(chunks):
            l1(c, g).start()

    for c in range(chunks):
        errors = tuple(jnp.zeros((rows, cells), jnp.float32) for _ in range(nq - 1))
        for g in range(groups):
            l1(c, g).wait_recv()

            def plane(i, errors, g=g, c=c):
                z = g * zg + i
                left = []
                for d in range(1, nq):
                    q = quad(d)
                    v = keep[c, q, z] + recv1[c, q, z] + errors[d - 1]
                    b = v.astype(jnp.bfloat16)
                    l2send[c, d - 1, z] = b
                    left.append(v - b.astype(jnp.float32))
                srcx[c, h + z] = keep[c, p, z] + recv1[c, p, z]
                return tuple(left)

            errors = lax.fori_loop(0, zg, plane, errors)
            for d in range(1, nq):
                l2(c, g, d).start()

    halo_wait_recv(*open_args)

    def outer(x):
        return pltpu.roll(x, cells - 1, x.ndim - 1)

    def inner(x):
        return pltpu.roll(x, 1, x.ndim - 1)

    c_out, c_in, f_out, f_in = (
        jnp.concatenate([coef_ref[i]] * (rows // 8), 0) for i in range(4)
    )

    def open_at(z, count):
        o = openx[pl.ds(z, count)]
        return jnp.concatenate([o] * (rows // 8), 1)

    for c in range(chunks):
        def gather_source(i, _, c=c):
            s = srcx[c, h + i]
            for d in range(1, nq):
                s = s + l2recv[c, d - 1, i].astype(jnp.float32)
            srcx[c, h + i] = s * PHI ** (-0.5)
            return 0

        for g in range(groups):
            for d in range(1, nq):
                l2(c, g, d).wait_recv()
            lax.fori_loop(g * zg, (g + 1) * zg, gather_source, 0)
        halo_args = (srcx.at[c], h, srcx.at[c], ha_s.at[c], ha_r.at[c])
        halo_send(*halo_args)
        halo_wait_recv(*halo_args)
        halo_wait_send(*halo_args)
        inv = inv_ref[c]

        def begin(i, _, c=c, inv=inv):
            z = i * 4
            pa[pl.ds(z, 4)] = open_at(z, 4) * inv * srcx[c, pl.ds(z, 4)]
            return 0

        lax.fori_loop(0, (depth + 2 * h) // 4, begin, 0)
        now, later = pa, pb
        for sweep in range(SWEEPS):
            first, length = sweep + 1, depth + 2 * (h - sweep - 1)
            step = 4 if length % 4 == 0 else 2

            def relax(i, _, c=c, inv=inv, now=now, later=later, first=first, step=step):
                z = first + i * step
                mid = now[pl.ds(z, step)]
                near = now[pl.ds(z + 1, step)] + now[pl.ds(z - 1, step)]
                near = near + (c_out * outer(mid) + c_in * inner(mid))
                new = open_at(z, step) * inv * (srcx[c, pl.ds(z, step)] + near)
                later[pl.ds(z, step)] = new
                return 0

            lax.fori_loop(0, length // step, relax, 0)
            now, later = later, now

        def suffix(i, acc, c=c, now=now):
            z = depth - 1 - i
            x = now[h + z]
            pot_ref[z, pl.ds(c * rows, rows)] = x
            acc = acc + (f_out * outer(x) - f_in * inner(x))
            loc[c, z] = acc
            return acc

        tot[c] = lax.fori_loop(0, depth, suffix, jnp.zeros((rows, cells), jnp.float32))
        for d in range(1, ngz):
            total(c, d).start()
        before = jnp.zeros((rows, cells), jnp.float32)
        for d in range(1, ngz):
            total(c, d).wait_recv()
            sender = lax.rem(gz - d + ngz, ngz)
            before = before + trecv[c, d - 1] * jnp.where(sender > gz, 1.0, 0.0)
        mine = pl.multiple_of(me * mode_rows + c * rows, rows)

        def shift(i, _, c=c, before=before, mine=mine):
            value = (loc[c, i] + before) * (ngz * depth) ** (-0.5)
            ms_ref[i, pl.ds(mine, rows), :] = value.astype(jnp.bfloat16)
            return 0

        lax.fori_loop(0, depth, shift, 0)
        for d in range(1, nq):
            gather(c, d).start()
        gather_sib(c).start()

    for c in range(chunks):
        for d in range(1, nq):
            gather(c, d).wait_recv()
            forward(c, d).start()
    for c in range(chunks):
        gather_sib(c).wait()
        for d in range(1, nq):
            gather(c, d).wait_send()
            forward(c, d).wait()
        for d in range(1, ngz):
            total(c, d).wait_send()
        for g in range(groups):
            l1(c, g).wait_send()
            for d in range(1, nq):
                l2(c, g, d).wait_send()
    halo_wait_send(*open_args)


def on_device(charge, orders, electrode):
    phi_rows, depth, cells = charge.shape
    n, ngz = lax.axis_size("phi"), lax.axis_size("gz")
    nq = n // 2
    mode_rows = MODES // n
    rows = 16 if mode_rows % 16 == 0 else mode_rows
    chunks = mode_rows // rows
    groups = 4
    me = lax.axis_index("phi")
    core = me % 2

    positions = me * phi_rows + jnp.arange(phi_rows, dtype=jnp.int32)
    phase_int = orders[:, None] * positions[None, :] % PHI
    angles = phase_int.astype(jnp.float32) * (2.0 * math.pi / PHI)
    table = jnp.concatenate([jnp.cos(angles), jnp.sin(angles)], 0).astype(jnp.bfloat16)
    blocks = table.reshape(nq, 2, chunks, rows, phi_rows)
    swapped = jnp.where(core == 0, blocks[:, ::-1], blocks)
    basis = swapped.transpose(1, 2, 0, 3, 4).reshape(MODES, phi_rows)

    mode_ids = me * mode_rows + jnp.arange(mode_rows, dtype=jnp.int32)
    matches = mode_ids[:, None] % ORDERS == jnp.arange(ORDERS, dtype=jnp.int32)[None, :]
    values = jnp.sum(jnp.where(matches, orders[None, :], 0), 1).astype(jnp.float32)
    cell = jnp.arange(cells, dtype=jnp.int32)
    radius = cell.astype(jnp.float32) + (cells // 2 + 0.5)
    inv = 1.0 / (4.0 + (values[:, None] / radius[None, :]) ** 2)
    inv = inv.reshape(chunks, rows, cells)
    not_last = (cell < cells - 1).astype(jnp.float32)
    not_first = (cell > 0).astype(jnp.float32)
    coef = jnp.stack(
        [
            (1.0 + 0.5 / radius) * not_last,
            (1.0 - 0.5 / radius) * not_first,
            0.5 * not_last,
            0.5 * not_first,
        ]
    )
    coef = jnp.broadcast_to(coef[:, None], (4, 8, cells))
    open_cells = (1 - electrode).astype(jnp.float32)
    open_cells = jnp.broadcast_to(open_cells[:, None], (depth, 8, cells))

    f32, bf16 = jnp.float32, jnp.bfloat16
    wide = depth + 2 * SWEEPS
    sem = pltpu.SemaphoreType.DMA
    vmem = pl.BlockSpec(memory_space=pltpu.VMEM)
    others = nq - 1
    potential, shifts = pl.pallas_call(
        functools.partial(kernel, n, ngz, chunks, groups),
        out_shape=(
            jax.ShapeDtypeStruct((depth, mode_rows, cells), f32),
            jax.ShapeDtypeStruct((depth, MODES, cells), bf16),
        ),
        in_specs=[vmem] * 5,
        out_specs=(vmem, vmem),
        scratch_shapes=[
            pltpu.VMEM((chunks, nq, depth, rows, cells), f32),
            pltpu.VMEM((chunks, nq, depth, rows, cells), f32),
            pltpu.VMEM((chunks, nq, depth, rows, cells), f32),
            pltpu.VMEM((chunks, others, depth, rows, cells), bf16),
            pltpu.VMEM((chunks, others, depth, rows, cells), bf16),
            pltpu.VMEM((wide, 8, cells), f32),
            pltpu.VMEM((chunks, wide, rows, cells), f32),
            pltpu.VMEM((wide, rows, cells), f32),
            pltpu.VMEM((wide, rows, cells), f32),
            pltpu.VMEM((chunks, depth, rows, cells), f32),
            pltpu.VMEM((chunks, rows, cells), f32),
            pltpu.VMEM((chunks, ngz - 1, rows, cells), f32),
            sem((chunks, groups)), sem((chunks, groups)),
            sem((chunks, groups, others)), sem((chunks, groups, others)),
            sem((2,)), sem((2,)),
            sem((chunks, 2)), sem((chunks, 2)),
            sem((chunks, ngz - 1)), sem((chunks, ngz - 1)),
            sem((chunks, others)), sem((chunks, others)),
            sem((chunks,)), sem((chunks,)),
            sem((chunks, others)), sem((chunks, others)),
        ],
        compiler_params=pltpu.CompilerParams(
            collective_id=0, has_side_effects=True, vmem_limit_bytes=48 * 1024 * 1024
        ),
    )(basis, charge.transpose(1, 0, 2), open_cells, inv, coef)

    running = jnp.einsum("mp,zmr->pzr", table, shifts, preferred_element_type=f32)
    distortion = (running * MODES ** (-0.5)).astype(bf16)
    return (distortion, potential.transpose(1, 0, 2))


def solution(mesh):
    return jax.shard_map(
        on_device,
        mesh=mesh,
        in_specs=(P(("grp", "phi"), "gz", None), P(), P("gz", None)),
        out_specs=(P(("grp", "phi"), "gz", None), P(("grp", "phi"), "gz", None)),
        check_vma=False,
    )
```

```python
import functools
import math

import jax
import jax.numpy as jnp
from jax import lax
from jax.experimental import pallas as pl
from jax.experimental.pallas import tpu as pltpu
from jax.sharding import PartitionSpec as P

PHI = 1024
ORDERS = 64
MODES = 128
SWEEPS = 4
MESH = pl.DeviceIdType.MESH


def kernel(
    n, ngz, chunks, groups,
    basis_ref, ch_ref, open_ref, inv_ref, coef_ref,
    pot_ref, ms_ref,
    send1, keep, recv1, l2send, l2recv, openx, srcx, wx, pa, pb, loc, tot, trecv,
    l1_s, l1_r, l2_s, l2_r, op_s, op_r, ha_s, ha_r, to_s, to_r, ag_s, ag_r, sb_s, sb_r, fw_s, fw_r,
):
    nq = n // 2
    depth, _, cells = ch_ref.shape
    rows = inv_ref.shape[1]
    mode_rows = chunks * rows
    zg = depth // groups
    h = SWEEPS
    me = lax.axis_index("phi")
    gz = lax.axis_index("gz")
    p, core = me // 2, lax.rem(me, 2)
    sib = p * 2 + 1 - core

    def remote(src, dst, s, r, where):
        return pltpu.make_async_remote_copy(
            src_ref=src, dst_ref=dst, send_sem=s, recv_sem=r, device_id=where, device_id_type=MESH
        )

    def quad(d):
        return lax.rem(p + d, nq)

    def slab(d):
        return lax.rem(gz + d, ngz)

    barrier = pltpu.get_barrier_semaphore()
    pl.semaphore_signal(barrier, inc=1, device_id={"phi": sib}, device_id_type=MESH)
    for d in range(1, nq):
        pl.semaphore_signal(
            barrier, inc=1, device_id={"phi": quad(d) * 2 + core}, device_id_type=MESH
        )
    for d in range(1, ngz):
        pl.semaphore_signal(barrier, inc=1, device_id={"gz": slab(d)}, device_id_type=MESH)

    def l1(c, g):
        part = (c, slice(None), pl.ds(g * zg, zg))
        return remote(send1.at[part], recv1.at[part], l1_s.at[c, g], l1_r.at[c, g], {"phi": sib})

    def l2(c, g, d):
        part = (c, d - 1, pl.ds(g * zg, zg))
        return remote(
            l2send.at[part], l2recv.at[part], l2_s.at[c, g, d - 1], l2_r.at[c, g, d - 1],
            {"phi": quad(d) * 2 + core},
        )

    def both_ways(action):
        @pl.when(gz > 0)
        def _():
            action(0, gz - 1)

        @pl.when(gz < ngz - 1)
        def _():
            action(1, gz + 1)

    def halo(buf_src, first, buf_dst, s, r, way, where):
        src = pl.ds(first, h) if way == 0 else pl.ds(first + depth - h, h)
        dst = pl.ds(h + depth, h) if way == 0 else pl.ds(0, h)
        return remote(buf_src.at[src], buf_dst.at[dst], s.at[way], r.at[way], {"gz": where})

    def halo_send(*args):
        both_ways(lambda way, where: halo(*args, way, where).start())

    def halo_wait_send(*args):
        both_ways(lambda way, where: halo(*args, way, where).wait_send())

    def halo_wait_recv(*args):
        both_ways(lambda way, where: halo(*args, 1 - way, where).wait_recv())

    def total(c, d):
        return remote(
            tot.at[c], trecv.at[c, d - 1], to_s.at[c, d - 1], to_r.at[c, d - 1], {"gz": slab(d)}
        )

    def block(owner, c):
        start = pl.multiple_of(owner * mode_rows + c * rows, rows)
        return ms_ref.at[:, pl.ds(start, rows), :]

    def gather(c, d):
        b = block(me, c)
        return remote(b, b, ag_s.at[c, d - 1], ag_r.at[c, d - 1], {"phi": quad(d) * 2 + core})

    def gather_sib(c):
        b = block(me, c)
        return remote(b, b, sb_s.at[c], sb_r.at[c], {"phi": sib})

    def forward(c, d):
        b = block(lax.rem(p - d + nq, nq) * 2 + core, c)
        return remote(b, b, fw_s.at[c, d - 1], fw_r.at[c, d - 1], {"phi": sib})

    openx[pl.ds(h, depth)] = open_ref[...]
    edge = jnp.zeros((h,) + srcx.shape[2:], jnp.float32)

    def no_slab(first):
        openx[pl.ds(first, h)] = jnp.zeros((h,) + openx.shape[1:], jnp.float32)
        for c in range(chunks):
            srcx[c, pl.ds(first, h)] = edge

    @pl.when(gz == 0)
    def _():
        no_slab(0)

    @pl.when(gz == ngz - 1)
    def _():
        no_slab(h + depth)

    pl.semaphore_wait(barrier, nq + ngz - 1)
    open_args = (open_ref, 0, openx, op_s, op_r)
    halo_send(*open_args)

    for g in range(groups):
        def plane(i, _, g=g):
            z = g * zg + i
            full = jnp.dot(basis_ref[...], ch_ref[z], preferred_element_type=jnp.float32)
            at = 0
            for buf in (send1, keep):
                for c in range(chunks):
                    for q in range(nq):
                        buf[c, q, z] = full[at : at + rows]
                        at += rows
            return 0

        lax.fori_loop(0, zg, plane, 0, unroll=True)
        for c in range(chunks):
            l1(c, g).start()

    for c in range(chunks):
        errors = tuple(jnp.zeros((rows, cells), jnp.float32) for _ in range(nq - 1))
        for g in range(groups):
            l1(c, g).wait_recv()

            def plane(i, errors, g=g, c=c):
                z = g * zg + i
                left = []
                for d in range(1, nq):
                    q = quad(d)
                    v = keep[c, q, z] + recv1[c, q, z] + errors[d - 1]
                    b = v.astype(jnp.bfloat16)
                    l2send[c, d - 1, z] = b
                    left.append(v - b.astype(jnp.float32))
                srcx[c, h + z] = keep[c, p, z] + recv1[c, p, z]
                return tuple(left)

            errors = lax.fori_loop(0, zg, plane, errors, unroll=True)
            for d in range(1, nq):
                l2(c, g, d).start()

    halo_wait_recv(*open_args)

    def outer(x):
        return pltpu.roll(x, cells - 1, x.ndim - 1)

    def inner(x):
        return pltpu.roll(x, 1, x.ndim - 1)

    c_out, c_in, f_out, f_in = (
        jnp.concatenate([coef_ref[i]] * (rows // 8), 0) for i in range(4)
    )

    def open_at(z, count):
        o = openx[pl.ds(z, count)]
        return jnp.concatenate([o] * (rows // 8), 1)

    for c in range(chunks):
        def gather_source(i, _, c=c):
            s = srcx[c, h + i]
            for d in range(1, nq):
                s = s + l2recv[c, d - 1, i].astype(jnp.float32)
            srcx[c, h + i] = s * PHI ** (-0.5)
            return 0

        for g in range(groups):
            for d in range(1, nq):
                l2(c, g, d).wait_recv()
            lax.fori_loop(g * zg, (g + 1) * zg, gather_source, 0, unroll=True)
        halo_args = (srcx.at[c], h, srcx.at[c], ha_s.at[c], ha_r.at[c])
        halo_send(*halo_args)
        halo_wait_recv(*halo_args)
        halo_wait_send(*halo_args)
        inv = inv_ref[c]

        def begin(i, _, c=c, inv=inv):
            z = i * 4
            weight = open_at(z, 4) * inv
            wx[pl.ds(z, 4)] = weight
            pa[pl.ds(z, 4)] = weight * srcx[c, pl.ds(z, 4)]
            return 0

        lax.fori_loop(0, (depth + 2 * h) // 4, begin, 0, unroll=2)
        now, later = pa, pb
        for sweep in range(SWEEPS):
            first, length = sweep + 1, depth + 2 * (h - sweep - 1)

            def relax(i, _, c=c, now=now, later=later, first=first):
                z = first + i
                mid = now[z]
                near = now[z + 1] + now[z - 1]
                near = near + (c_out * outer(mid) + c_in * inner(mid))
                later[z] = wx[z] * (srcx[c, z] + near)
                return 0

            lax.fori_loop(0, length, relax, 0, unroll=length // 2)
            now, later = later, now

        def suffix(i, acc, c=c, now=now):
            z = depth - 1 - i
            x = now[h + z]
            pot_ref[z, pl.ds(c * rows, rows)] = x
            acc = acc + (f_out * outer(x) - f_in * inner(x))
            loc[c, z] = acc
            return acc

        tot[c] = lax.fori_loop(0, depth, suffix, jnp.zeros((rows, cells), jnp.float32), unroll=8)
        for d in range(1, ngz):
            total(c, d).start()
        before = jnp.zeros((rows, cells), jnp.float32)
        for d in range(1, ngz):
            total(c, d).wait_recv()
            sender = lax.rem(gz - d + ngz, ngz)
            before = before + trecv[c, d - 1] * jnp.where(sender > gz, 1.0, 0.0)
        mine = pl.multiple_of(me * mode_rows + c * rows, rows)

        def shift(i, _, c=c, before=before, mine=mine):
            value = (loc[c, i] + before) * (ngz * depth) ** (-0.5)
            ms_ref[i, pl.ds(mine, rows), :] = value.astype(jnp.bfloat16)
            return 0

        lax.fori_loop(0, depth, shift, 0, unroll=8)
        for d in range(1, nq):
            gather(c, d).start()
        gather_sib(c).start()

    for c in range(chunks):
        for d in range(1, nq):
            gather(c, d).wait_recv()
            forward(c, d).start()
    for c in range(chunks):
        gather_sib(c).wait()
        for d in range(1, nq):
            gather(c, d).wait_send()
            forward(c, d).wait()
        for d in range(1, ngz):
            total(c, d).wait_send()
        for g in range(groups):
            l1(c, g).wait_send()
            for d in range(1, nq):
                l2(c, g, d).wait_send()
    halo_wait_send(*open_args)


def synthesize(weight_ref, shift_ref, out_ref, wide_ref):
    for z in range(shift_ref.shape[0]):
        wide_ref[:, z, :] = jnp.dot(
            weight_ref[...], shift_ref[z], preferred_element_type=jnp.float32
        )
    step = 16

    def narrow(i, _):
        at = pl.ds(i * step, step)
        out_ref[at] = (wide_ref[at] * MODES ** (-0.5)).astype(jnp.bfloat16)
        return 0

    lax.fori_loop(0, wide_ref.shape[0] // step, narrow, 0)


def on_device(charge, orders, electrode):
    phi_rows, depth, cells = charge.shape
    n, ngz = lax.axis_size("phi"), lax.axis_size("gz")
    nq = n // 2
    mode_rows = MODES // n
    rows = 16 if mode_rows % 16 == 0 else mode_rows
    chunks = mode_rows // rows
    groups = 4
    me = lax.axis_index("phi")
    core = me % 2

    positions = me * phi_rows + jnp.arange(phi_rows, dtype=jnp.int32)
    phase_int = orders[:, None] * positions[None, :] % PHI
    angles = phase_int.astype(jnp.float32) * (2.0 * math.pi / PHI)
    table = jnp.concatenate([jnp.cos(angles), jnp.sin(angles)], 0).astype(jnp.bfloat16)
    blocks = table.reshape(nq, 2, chunks, rows, phi_rows)
    swapped = jnp.where(core == 0, blocks[:, ::-1], blocks)
    basis = swapped.transpose(1, 2, 0, 3, 4).reshape(MODES, phi_rows)

    mode_ids = me * mode_rows + jnp.arange(mode_rows, dtype=jnp.int32)
    matches = mode_ids[:, None] % ORDERS == jnp.arange(ORDERS, dtype=jnp.int32)[None, :]
    values = jnp.sum(jnp.where(matches, orders[None, :], 0), 1).astype(jnp.float32)
    cell = jnp.arange(cells, dtype=jnp.int32)
    radius = cell.astype(jnp.float32) + (cells // 2 + 0.5)
    inv = 1.0 / (4.0 + (values[:, None] / radius[None, :]) ** 2)
    inv = inv.reshape(chunks, rows, cells)
    not_last = (cell < cells - 1).astype(jnp.float32)
    not_first = (cell > 0).astype(jnp.float32)
    coef = jnp.stack(
        [
            (1.0 + 0.5 / radius) * not_last,
            (1.0 - 0.5 / radius) * not_first,
            0.5 * not_last,
            0.5 * not_first,
        ]
    )
    coef = jnp.broadcast_to(coef[:, None], (4, 8, cells))
    open_cells = (1 - electrode).astype(jnp.float32)
    open_cells = jnp.broadcast_to(open_cells[:, None], (depth, 8, cells))

    f32, bf16 = jnp.float32, jnp.bfloat16
    wide = depth + 2 * SWEEPS
    sem = pltpu.SemaphoreType.DMA
    vmem = pl.BlockSpec(memory_space=pltpu.VMEM)
    others = nq - 1
    potential, shifts = pl.pallas_call(
        functools.partial(kernel, n, ngz, chunks, groups),
        out_shape=(
            jax.ShapeDtypeStruct((depth, mode_rows, cells), f32),
            jax.ShapeDtypeStruct((depth, MODES, cells), bf16),
        ),
        in_specs=[vmem] * 5,
        out_specs=(vmem, vmem),
        scratch_shapes=[
            pltpu.VMEM((chunks, nq, depth, rows, cells), f32),
            pltpu.VMEM((chunks, nq, depth, rows, cells), f32),
            pltpu.VMEM((chunks, nq, depth, rows, cells), f32),
            pltpu.VMEM((chunks, others, depth, rows, cells), bf16),
            pltpu.VMEM((chunks, others, depth, rows, cells), bf16),
            pltpu.VMEM((wide, 8, cells), f32),
            pltpu.VMEM((chunks, wide, rows, cells), f32),
            pltpu.VMEM((wide, rows, cells), f32),
            pltpu.VMEM((wide, rows, cells), f32),
            pltpu.VMEM((wide, rows, cells), f32),
            pltpu.VMEM((chunks, depth, rows, cells), f32),
            pltpu.VMEM((chunks, rows, cells), f32),
            pltpu.VMEM((chunks, ngz - 1, rows, cells), f32),
            sem((chunks, groups)), sem((chunks, groups)),
            sem((chunks, groups, others)), sem((chunks, groups, others)),
            sem((2,)), sem((2,)),
            sem((chunks, 2)), sem((chunks, 2)),
            sem((chunks, ngz - 1)), sem((chunks, ngz - 1)),
            sem((chunks, others)), sem((chunks, others)),
            sem((chunks,)), sem((chunks,)),
            sem((chunks, others)), sem((chunks, others)),
        ],
        compiler_params=pltpu.CompilerParams(
            collective_id=0, has_side_effects=True, vmem_limit_bytes=48 * 1024 * 1024
        ),
    )(basis, charge.transpose(1, 0, 2), open_cells, inv, coef)

    part = 16
    distortion = pl.pallas_call(
        synthesize,
        grid=(depth // part,),
        out_shape=jax.ShapeDtypeStruct((phi_rows, depth, cells), bf16),
        in_specs=[
            pl.BlockSpec((phi_rows, MODES), lambda i: (0, 0)),
            pl.BlockSpec((part, MODES, cells), lambda i: (i, 0, 0)),
        ],
        out_specs=pl.BlockSpec((phi_rows, part, cells), lambda i: (0, i, 0)),
        scratch_shapes=[pltpu.VMEM((phi_rows, part, cells), f32)],
        compiler_params=pltpu.CompilerParams(vmem_limit_bytes=32 * 1024 * 1024),
    )(table.T, shifts)
    return (distortion, potential.transpose(1, 0, 2))


def solution(mesh):
    return jax.shard_map(
        on_device,
        mesh=mesh,
        in_specs=(P(("grp", "phi"), "gz", None), P(), P("gz", None)),
        out_specs=(P(("grp", "phi"), "gz", None), P(("grp", "phi"), "gz", None)),
        check_vma=False,
    )
```

```python
import functools
import math

import jax
import jax.numpy as jnp
from jax import lax
from jax.experimental import pallas as pl
from jax.experimental.pallas import tpu as pltpu
from jax.sharding import PartitionSpec as P

PHI = 1024
ORDERS = 64
MODES = 128
SWEEPS = 4
MESH = pl.DeviceIdType.MESH


def kernel(
    n, ngz, chunks, groups,
    basis_ref, charge_ref, open_ref, inv_ref, coef_ref,
    pot_ref, ms_ref,
    ch, chf, ch_s, send1, keep, recv1, l2send, l2recv, openx, srcx, wx, pa, pb, loc, tot, trecv,
    l1_s, l1_r, l2_s, l2_r, op_s, op_r, ha_s, ha_r, to_s, to_r, ag_s, ag_r, sb_s, sb_r, fw_s, fw_r,
):
    nq = n // 2
    _, depth, cells = charge_ref.shape
    part = ch.shape[2]
    rows = inv_ref.shape[1]
    mode_rows = chunks * rows
    zg = depth // groups
    h = SWEEPS
    me = lax.axis_index("phi")
    gz = lax.axis_index("gz")
    p, core = me // 2, lax.rem(me, 2)
    sib = p * 2 + 1 - core

    def remote(src, dst, s, r, where):
        return pltpu.make_async_remote_copy(
            src_ref=src, dst_ref=dst, send_sem=s, recv_sem=r, device_id=where, device_id_type=MESH
        )

    def quad(d):
        return lax.rem(p + d, nq)

    def slab(d):
        return lax.rem(gz + d, ngz)

    def load(j):
        src = charge_ref.at[:, pl.ds(j * part, part), :]
        return pltpu.make_async_copy(src, ch.at[j], ch_s.at[j])

    for j in range(depth // part):
        load(j).start()
    barrier = pltpu.get_barrier_semaphore()
    pl.semaphore_signal(barrier, inc=1, device_id={"phi": sib}, device_id_type=MESH)
    for d in range(1, nq):
        pl.semaphore_signal(
            barrier, inc=1, device_id={"phi": quad(d) * 2 + core}, device_id_type=MESH
        )
    for d in range(1, ngz):
        pl.semaphore_signal(barrier, inc=1, device_id={"gz": slab(d)}, device_id_type=MESH)

    def l1(c, g):
        part = (c, slice(None), pl.ds(g * zg, zg))
        return remote(send1.at[part], recv1.at[part], l1_s.at[c, g], l1_r.at[c, g], {"phi": sib})

    def l2(c, g, d):
        part = (c, d - 1, pl.ds(g * zg, zg))
        return remote(
            l2send.at[part], l2recv.at[part], l2_s.at[c, g, d - 1], l2_r.at[c, g, d - 1],
            {"phi": quad(d) * 2 + core},
        )

    def both_ways(action):
        @pl.when(gz > 0)
        def _():
            action(0, gz - 1)

        @pl.when(gz < ngz - 1)
        def _():
            action(1, gz + 1)

    def halo(buf_src, first, buf_dst, s, r, way, where):
        src = pl.ds(first, h) if way == 0 else pl.ds(first + depth - h, h)
        dst = pl.ds(h + depth, h) if way == 0 else pl.ds(0, h)
        return remote(buf_src.at[src], buf_dst.at[dst], s.at[way], r.at[way], {"gz": where})

    def halo_send(*args):
        both_ways(lambda way, where: halo(*args, way, where).start())

    def halo_wait_send(*args):
        both_ways(lambda way, where: halo(*args, way, where).wait_send())

    def halo_wait_recv(*args):
        both_ways(lambda way, where: halo(*args, 1 - way, where).wait_recv())

    def total(c, d):
        return remote(
            tot.at[c], trecv.at[c, d - 1], to_s.at[c, d - 1], to_r.at[c, d - 1], {"gz": slab(d)}
        )

    def block(owner, c):
        start = pl.multiple_of(owner * mode_rows + c * rows, rows)
        return ms_ref.at[:, pl.ds(start, rows), :]

    def gather(c, d):
        b = block(me, c)
        return remote(b, b, ag_s.at[c, d - 1], ag_r.at[c, d - 1], {"phi": quad(d) * 2 + core})

    def gather_sib(c):
        b = block(me, c)
        return remote(b, b, sb_s.at[c], sb_r.at[c], {"phi": sib})

    def forward(c, d):
        b = block(lax.rem(p - d + nq, nq) * 2 + core, c)
        return remote(b, b, fw_s.at[c, d - 1], fw_r.at[c, d - 1], {"phi": sib})

    openx[pl.ds(h, depth)] = open_ref[...]
    edge = jnp.zeros((h,) + srcx.shape[2:], jnp.float32)

    def no_slab(first):
        openx[pl.ds(first, h)] = jnp.zeros((h,) + openx.shape[1:], jnp.float32)
        for c in range(chunks):
            srcx[c, pl.ds(first, h)] = edge

    @pl.when(gz == 0)
    def _():
        no_slab(0)

    @pl.when(gz == ngz - 1)
    def _():
        no_slab(h + depth)

    pl.semaphore_wait(barrier, nq + ngz - 1)
    open_args = (open_ref, 0, openx, op_s, op_r)
    halo_send(*open_args)

    def round_group(c, g, errors):
        l1(c, g).wait_recv()

        def plane(i, errors):
            z = g * zg + i
            left = []
            for d in range(1, nq):
                q = quad(d)
                v = keep[c, q, z] + recv1[c, q, z] + errors[d - 1]
                b = v.astype(jnp.bfloat16)
                l2send[c, d - 1, z] = b
                left.append(v - b.astype(jnp.float32))
            srcx[c, h + z] = keep[c, p, z] + recv1[c, p, z]
            return tuple(left)

        errors = lax.fori_loop(0, zg, plane, errors, unroll=True)
        for d in range(1, nq):
            l2(c, g, d).start()
        return errors

    no_errors = tuple(jnp.zeros((rows, cells), jnp.float32) for _ in range(nq - 1))
    errors = no_errors
    for g in range(groups):
        j = g * zg // part
        if g * zg % part == 0:
            load(j).wait()

            def widen(i, _, j=j):
                at = pl.ds(i * 8, 8)
                chf[at] = ch[j, at].astype(jnp.float32)
                return 0

            lax.fori_loop(0, chf.shape[0] // 8, widen, 0)

        def plane(i, _, g=g, j=j):
            z = g * zg + i
            here = chf[:, g * zg - j * part + i, :].astype(jnp.bfloat16)
            full = jnp.dot(basis_ref[...], here, preferred_element_type=jnp.float32)
            at = 0
            for buf in (send1, keep):
                for c in range(chunks):
                    for q in range(nq):
                        buf[c, q, z] = full[at : at + rows]
                        at += rows
            return 0

        lax.fori_loop(0, zg, plane, 0, unroll=True)
        for c in range(chunks):
            l1(c, g).start()

        if g > 0:
            errors = round_group(0, g - 1, errors)
    round_group(0, groups - 1, errors)
    for c in range(1, chunks):
        errors = no_errors
        for g in range(groups):
            errors = round_group(c, g, errors)

    halo_wait_recv(*open_args)

    def outer(x):
        return pltpu.roll(x, cells - 1, x.ndim - 1)

    def inner(x):
        return pltpu.roll(x, 1, x.ndim - 1)

    c_out, c_in, f_out, f_in = (
        jnp.concatenate([coef_ref[i]] * (rows // 8), 0) for i in range(4)
    )

    def open_at(z, count):
        o = openx[pl.ds(z, count)]
        return jnp.concatenate([o] * (rows // 8), 1)

    def halo_of(c):
        return (srcx.at[c], h, srcx.at[c], ha_s.at[c], ha_r.at[c])

    def sources(c):
        def gather_source(i, _):
            s = srcx[c, h + i]
            for d in range(1, nq):
                s = s + l2recv[c, d - 1, i].astype(jnp.float32)
            srcx[c, h + i] = s * PHI ** (-0.5)
            return 0

        for g in range(groups):
            for d in range(1, nq):
                l2(c, g, d).wait_recv()
            lax.fori_loop(g * zg, (g + 1) * zg, gather_source, 0, unroll=True)
        halo_send(*halo_of(c))

    sources(0)
    for c in range(chunks):
        halo_wait_recv(*halo_of(c))
        inv = inv_ref[c]

        def begin(i, _, c=c, inv=inv):
            z = i * 4
            weight = open_at(z, 4) * inv
            wx[pl.ds(z, 4)] = weight
            pa[pl.ds(z, 4)] = weight * srcx[c, pl.ds(z, 4)]
            return 0

        lax.fori_loop(0, (depth + 2 * h) // 4, begin, 0, unroll=2)
        now, later = pa, pb
        for sweep in range(SWEEPS):
            first, length = sweep + 1, depth + 2 * (h - sweep - 1)

            def relax(i, _, c=c, now=now, later=later, first=first):
                z = first + i
                mid = now[z]
                near = now[z + 1] + now[z - 1]
                near = near + (c_out * outer(mid) + c_in * inner(mid))
                later[z] = wx[z] * (srcx[c, z] + near)
                return 0

            lax.fori_loop(0, length, relax, 0, unroll=length // 2)
            now, later = later, now

        def suffix(i, acc, c=c, now=now):
            z = depth - 1 - i
            x = now[h + z]
            pot_ref[z, pl.ds(c * rows, rows)] = x
            acc = acc + (f_out * outer(x) - f_in * inner(x))
            loc[c, z] = acc
            return acc

        tot[c] = lax.fori_loop(0, depth, suffix, jnp.zeros((rows, cells), jnp.float32), unroll=8)
        for d in range(1, ngz):
            total(c, d).start()
        if c + 1 < chunks:
            sources(c + 1)
        before = jnp.zeros((rows, cells), jnp.float32)
        for d in range(1, ngz):
            total(c, d).wait_recv()
            sender = lax.rem(gz - d + ngz, ngz)
            before = before + trecv[c, d - 1] * jnp.where(sender > gz, 1.0, 0.0)
        mine = pl.multiple_of(me * mode_rows + c * rows, rows)

        def shift(i, _, c=c, before=before, mine=mine):
            value = (loc[c, i] + before) * (ngz * depth) ** (-0.5)
            ms_ref[i, pl.ds(mine, rows), :] = value.astype(jnp.bfloat16)
            return 0

        lax.fori_loop(0, depth, shift, 0, unroll=8)
        for d in range(1, nq):
            gather(c, d).start()
        gather_sib(c).start()

    for c in range(chunks):
        for d in range(1, nq):
            gather(c, d).wait_recv()
            forward(c, d).start()
    for c in range(chunks):
        gather_sib(c).wait()
        halo_wait_send(*halo_of(c))
        for d in range(1, nq):
            gather(c, d).wait_send()
            forward(c, d).wait()
        for d in range(1, ngz):
            total(c, d).wait_send()
        for g in range(groups):
            l1(c, g).wait_send()
            for d in range(1, nq):
                l2(c, g, d).wait_send()
    halo_wait_send(*open_args)


def synthesize(weight_ref, shift_ref, pot_ref, out_ref, turned_ref, wide_ref):
    for z in range(shift_ref.shape[0]):
        turned_ref[:, z, :] = pot_ref[z]
        wide_ref[:, z, :] = jnp.dot(
            weight_ref[...], shift_ref[z], preferred_element_type=jnp.float32
        )
    step = 16

    def narrow(i, _):
        at = pl.ds(i * step, step)
        out_ref[at] = (wide_ref[at] * MODES ** (-0.5)).astype(jnp.bfloat16)
        return 0

    lax.fori_loop(0, wide_ref.shape[0] // step, narrow, 0)


def on_device(charge, orders, electrode):
    phi_rows, depth, cells = charge.shape
    n, ngz = lax.axis_size("phi"), lax.axis_size("gz")
    nq = n // 2
    mode_rows = MODES // n
    rows = 16 if mode_rows % 16 == 0 else mode_rows
    chunks = mode_rows // rows
    groups, part = 4, 16
    me = lax.axis_index("phi")
    core = me % 2

    positions = me * phi_rows + jnp.arange(phi_rows, dtype=jnp.int32)
    phase_int = orders[:, None] * positions[None, :] % PHI
    angles = phase_int.astype(jnp.float32) * (2.0 * math.pi / PHI)
    table = jnp.concatenate([jnp.cos(angles), jnp.sin(angles)], 0).astype(jnp.bfloat16)
    blocks = table.reshape(nq, 2, chunks, rows, phi_rows)
    swapped = jnp.where(core == 0, blocks[:, ::-1], blocks)
    basis = swapped.transpose(1, 2, 0, 3, 4).reshape(MODES, phi_rows)

    mode_ids = me * mode_rows + jnp.arange(mode_rows, dtype=jnp.int32)
    matches = mode_ids[:, None] % ORDERS == jnp.arange(ORDERS, dtype=jnp.int32)[None, :]
    values = jnp.sum(jnp.where(matches, orders[None, :], 0), 1).astype(jnp.float32)
    cell = jnp.arange(cells, dtype=jnp.int32)
    radius = cell.astype(jnp.float32) + (cells // 2 + 0.5)
    inv = 1.0 / (4.0 + (values[:, None] / radius[None, :]) ** 2)
    inv = inv.reshape(chunks, rows, cells)
    not_last = (cell < cells - 1).astype(jnp.float32)
    not_first = (cell > 0).astype(jnp.float32)
    coef = jnp.stack(
        [
            (1.0 + 0.5 / radius) * not_last,
            (1.0 - 0.5 / radius) * not_first,
            0.5 * not_last,
            0.5 * not_first,
        ]
    )
    coef = jnp.broadcast_to(coef[:, None], (4, 8, cells))
    open_cells = (1 - electrode).astype(jnp.float32)
    open_cells = jnp.broadcast_to(open_cells[:, None], (depth, 8, cells))

    f32, bf16 = jnp.float32, jnp.bfloat16
    wide = depth + 2 * SWEEPS
    sem = pltpu.SemaphoreType.DMA
    vmem = pl.BlockSpec(memory_space=pltpu.VMEM)
    others = nq - 1
    potential, shifts = pl.pallas_call(
        functools.partial(kernel, n, ngz, chunks, groups),
        out_shape=(
            jax.ShapeDtypeStruct((depth, mode_rows, cells), f32),
            jax.ShapeDtypeStruct((depth, MODES, cells), bf16),
        ),
        in_specs=[vmem, pl.BlockSpec(memory_space=pl.ANY)] + [vmem] * 3,
        out_specs=(vmem, vmem),
        scratch_shapes=[
            pltpu.VMEM((depth // part, phi_rows, part, cells), bf16),
            pltpu.VMEM((phi_rows, part, cells), f32),
            sem((depth // part,)),
            pltpu.VMEM((chunks, nq, depth, rows, cells), f32),
            pltpu.VMEM((chunks, nq, depth, rows, cells), f32),
            pltpu.VMEM((chunks, nq, depth, rows, cells), f32),
            pltpu.VMEM((chunks, others, depth, rows, cells), bf16),
            pltpu.VMEM((chunks, others, depth, rows, cells), bf16),
            pltpu.VMEM((wide, 8, cells), f32),
            pltpu.VMEM((chunks, wide, rows, cells), f32),
            pltpu.VMEM((wide, rows, cells), f32),
            pltpu.VMEM((wide, rows, cells), f32),
            pltpu.VMEM((wide, rows, cells), f32),
            pltpu.VMEM((chunks, depth, rows, cells), f32),
            pltpu.VMEM((chunks, rows, cells), f32),
            pltpu.VMEM((chunks, ngz - 1, rows, cells), f32),
            sem((chunks, groups)), sem((chunks, groups)),
            sem((chunks, groups, others)), sem((chunks, groups, others)),
            sem((2,)), sem((2,)),
            sem((chunks, 2)), sem((chunks, 2)),
            sem((chunks, ngz - 1)), sem((chunks, ngz - 1)),
            sem((chunks, others)), sem((chunks, others)),
            sem((chunks,)), sem((chunks,)),
            sem((chunks, others)), sem((chunks, others)),
        ],
        compiler_params=pltpu.CompilerParams(
            collective_id=0, has_side_effects=True, vmem_limit_bytes=48 * 1024 * 1024
        ),
    )(basis, charge, open_cells, inv, coef)

    distortion, potential = pl.pallas_call(
        synthesize,
        grid=(depth // part,),
        out_shape=(
            jax.ShapeDtypeStruct((phi_rows, depth, cells), bf16),
            jax.ShapeDtypeStruct((mode_rows, depth, cells), f32),
        ),
        in_specs=[
            pl.BlockSpec((phi_rows, MODES), lambda i: (0, 0)),
            pl.BlockSpec((part, MODES, cells), lambda i: (i, 0, 0)),
            pl.BlockSpec((part, mode_rows, cells), lambda i: (i, 0, 0)),
        ],
        out_specs=(
            pl.BlockSpec((phi_rows, part, cells), lambda i: (0, i, 0)),
            pl.BlockSpec((mode_rows, part, cells), lambda i: (0, i, 0)),
        ),
        scratch_shapes=[pltpu.VMEM((phi_rows, part, cells), f32)],
        compiler_params=pltpu.CompilerParams(vmem_limit_bytes=32 * 1024 * 1024),
    )(table.T, shifts, potential)
    return (distortion, potential)


def solution(mesh):
    return jax.shard_map(
        on_device,
        mesh=mesh,
        in_specs=(P(("grp", "phi"), "gz", None), P(), P("gz", None)),
        out_specs=(P(("grp", "phi"), "gz", None), P(("grp", "phi"), "gz", None)),
        check_vma=False,
    )
```

```python
import functools
import math

import jax
import jax.numpy as jnp
from jax import lax
from jax.experimental import pallas as pl
from jax.experimental.pallas import tpu as pltpu
from jax.sharding import PartitionSpec as P

PHI = 1024
ORDERS = 64
MODES = 128
SWEEPS = 4
MESH = pl.DeviceIdType.MESH


def kernel(
    n, ngz, chunks, groups,
    basis_ref, charge_ref, open_ref, inv_ref, coef_ref,
    pot_ref, ms_ref,
    ch, chf, ch_s, send1, keep, recv1, l2send, l2recv, openx, srcx, wx, pa, pb, loc, tot, trecv,
    l1_s, l1_r, l2_s, l2_r, op_s, op_r, ha_s, ha_r, to_s, to_r, ag_s, ag_r, sb_s, sb_r, fw_s, fw_r,
):
    nq = n // 2
    _, depth, cells = charge_ref.shape
    part = ch.shape[2]
    rows = inv_ref.shape[1]
    mode_rows = chunks * rows
    zg = depth // groups
    h = SWEEPS
    me = lax.axis_index("phi")
    gz = lax.axis_index("gz")
    p, core = me // 2, lax.rem(me, 2)
    sib = p * 2 + 1 - core

    def remote(src, dst, s, r, where):
        return pltpu.make_async_remote_copy(
            src_ref=src, dst_ref=dst, send_sem=s, recv_sem=r, device_id=where, device_id_type=MESH
        )

    def quad(d):
        return lax.rem(p + d, nq)

    def slab(d):
        return lax.rem(gz + d, ngz)

    def load(j):
        src = charge_ref.at[:, pl.ds(j * part, part), :]
        return pltpu.make_async_copy(src, ch.at[j], ch_s.at[j])

    for j in range(depth // part):
        load(j).start()
    barrier = pltpu.get_barrier_semaphore()
    pl.semaphore_signal(barrier, inc=1, device_id={"phi": sib}, device_id_type=MESH)
    for d in range(1, nq):
        pl.semaphore_signal(
            barrier, inc=1, device_id={"phi": quad(d) * 2 + core}, device_id_type=MESH
        )
    for d in range(1, ngz):
        pl.semaphore_signal(barrier, inc=1, device_id={"gz": slab(d)}, device_id_type=MESH)

    def l1(c, g):
        part = (c, slice(None), pl.ds(g * zg, zg))
        return remote(send1.at[part], recv1.at[part], l1_s.at[c, g], l1_r.at[c, g], {"phi": sib})

    def l2(c, g, d):
        part = (c, d - 1, pl.ds(g * zg, zg))
        return remote(
            l2send.at[part], l2recv.at[part], l2_s.at[c, g, d - 1], l2_r.at[c, g, d - 1],
            {"phi": quad(d) * 2 + core},
        )

    def both_ways(action):
        @pl.when(gz > 0)
        def _():
            action(0, gz - 1)

        @pl.when(gz < ngz - 1)
        def _():
            action(1, gz + 1)

    def halo(buf_src, first, buf_dst, s, r, way, where):
        src = pl.ds(first, h) if way == 0 else pl.ds(first + depth - h, h)
        dst = pl.ds(h + depth, h) if way == 0 else pl.ds(0, h)
        return remote(buf_src.at[src], buf_dst.at[dst], s.at[way], r.at[way], {"gz": where})

    def halo_send(*args):
        both_ways(lambda way, where: halo(*args, way, where).start())

    def halo_wait_send(*args):
        both_ways(lambda way, where: halo(*args, way, where).wait_send())

    def halo_wait_recv(*args):
        both_ways(lambda way, where: halo(*args, 1 - way, where).wait_recv())

    def total(c, d):
        return remote(
            tot.at[c], trecv.at[c, d - 1], to_s.at[c, d - 1], to_r.at[c, d - 1], {"gz": slab(d)}
        )

    def block(owner, c):
        start = pl.multiple_of(owner * mode_rows + c * rows, rows)
        return ms_ref.at[:, pl.ds(start, rows), :]

    def gather(c, d):
        b = block(me, c)
        return remote(b, b, ag_s.at[c, d - 1], ag_r.at[c, d - 1], {"phi": quad(d) * 2 + core})

    def gather_sib(c):
        b = block(me, c)
        return remote(b, b, sb_s.at[c], sb_r.at[c], {"phi": sib})

    def forward(c, d):
        b = block(lax.rem(p - d + nq, nq) * 2 + core, c)
        return remote(b, b, fw_s.at[c, d - 1], fw_r.at[c, d - 1], {"phi": sib})

    openx[pl.ds(h, depth)] = open_ref[...]
    edge = jnp.zeros((h,) + srcx.shape[2:], jnp.float32)

    def no_slab(first):
        openx[pl.ds(first, h)] = jnp.zeros((h,) + openx.shape[1:], jnp.float32)
        for c in range(chunks):
            srcx[c, pl.ds(first, h)] = edge

    @pl.when(gz == 0)
    def _():
        no_slab(0)

    @pl.when(gz == ngz - 1)
    def _():
        no_slab(h + depth)

    open_args = (open_ref, 0, openx, op_s, op_r)

    def round_group(c, g, errors):
        l1(c, g).wait_recv()

        def plane(i, errors):
            z = g * zg + i
            left = []
            for d in range(1, nq):
                q = quad(d)
                v = keep[c, q, z] + recv1[c, q, z] + errors[d - 1]
                b = v.astype(jnp.bfloat16)
                l2send[c, d - 1, z] = b
                left.append(v - b.astype(jnp.float32))
            srcx[c, h + z] = keep[c, p, z] + recv1[c, p, z]
            return tuple(left)

        errors = lax.fori_loop(0, zg, plane, errors, unroll=True)
        for d in range(1, nq):
            l2(c, g, d).start()
        return errors

    no_errors = tuple(jnp.zeros((rows, cells), jnp.float32) for _ in range(nq - 1))
    errors = no_errors
    for g in range(groups):
        j = g * zg // part
        if g * zg % part == 0:
            load(j).wait()

            def widen(i, _, j=j):
                at = pl.ds(i * 8, 8)
                chf[at] = ch[j, at].astype(jnp.float32)
                return 0

            lax.fori_loop(0, chf.shape[0] // 8, widen, 0)

        def plane(i, _, g=g, j=j):
            z = g * zg + i
            here = chf[:, g * zg - j * part + i, :].astype(jnp.bfloat16)
            full = jnp.dot(basis_ref[...], here, preferred_element_type=jnp.float32)
            at = 0
            for buf in (send1, keep):
                for c in range(chunks):
                    for q in range(nq):
                        buf[c, q, z] = full[at : at + rows]
                        at += rows
            return 0

        lax.fori_loop(0, zg, plane, 0, unroll=True)
        if g == 0:
            pl.semaphore_wait(barrier, nq + ngz - 1)
            halo_send(*open_args)
        for c in range(chunks):
            l1(c, g).start()

        if g > 0:
            errors = round_group(0, g - 1, errors)
    round_group(0, groups - 1, errors)
    for c in range(1, chunks):
        errors = no_errors
        for g in range(groups):
            errors = round_group(c, g, errors)

    halo_wait_recv(*open_args)

    def outer(x):
        return pltpu.roll(x, cells - 1, x.ndim - 1)

    def inner(x):
        return pltpu.roll(x, 1, x.ndim - 1)

    c_out, c_in, f_out, f_in = (
        jnp.concatenate([coef_ref[i]] * (rows // 8), 0) for i in range(4)
    )

    def open_at(z, count):
        o = openx[pl.ds(z, count)]
        return jnp.concatenate([o] * (rows // 8), 1)

    def halo_of(c):
        return (srcx.at[c], h, srcx.at[c], ha_s.at[c], ha_r.at[c])

    def sources(c):
        def gather_source(i, _):
            s = srcx[c, h + i]
            for d in range(1, nq):
                s = s + l2recv[c, d - 1, i].astype(jnp.float32)
            srcx[c, h + i] = s * PHI ** (-0.5)
            return 0

        for g in range(groups):
            for d in range(1, nq):
                l2(c, g, d).wait_recv()
            lax.fori_loop(g * zg, (g + 1) * zg, gather_source, 0, unroll=True)
        halo_send(*halo_of(c))

    sources(0)
    for c in range(chunks):
        halo_wait_recv(*halo_of(c))
        inv = inv_ref[c]

        def begin(i, _, c=c, inv=inv):
            z = i * 4
            weight = open_at(z, 4) * inv
            wx[pl.ds(z, 4)] = weight
            pa[pl.ds(z, 4)] = weight * srcx[c, pl.ds(z, 4)]
            return 0

        lax.fori_loop(0, (depth + 2 * h) // 4, begin, 0, unroll=2)
        now, later = pa, pb
        for sweep in range(SWEEPS):
            first, length = sweep + 1, depth + 2 * (h - sweep - 1)

            def relax(i, _, c=c, now=now, later=later, first=first):
                z = first + i
                mid = now[z]
                near = now[z + 1] + now[z - 1]
                near = near + (c_out * outer(mid) + c_in * inner(mid))
                later[z] = wx[z] * (srcx[c, z] + near)
                return 0

            lax.fori_loop(0, length, relax, 0, unroll=length // 2)
            now, later = later, now

        def suffix(i, acc, c=c, now=now):
            z = depth - 1 - i
            x = now[h + z]
            pot_ref[z, pl.ds(c * rows, rows)] = x
            acc = acc + (f_out * outer(x) - f_in * inner(x))
            loc[c, z] = acc
            return acc

        tot[c] = lax.fori_loop(0, depth, suffix, jnp.zeros((rows, cells), jnp.float32), unroll=8)
        for d in range(1, ngz):
            total(c, d).start()
        if c + 1 < chunks:
            sources(c + 1)
        before = jnp.zeros((rows, cells), jnp.float32)
        for d in range(1, ngz):
            total(c, d).wait_recv()
            sender = lax.rem(gz - d + ngz, ngz)
            before = before + trecv[c, d - 1] * jnp.where(sender > gz, 1.0, 0.0)
        mine = pl.multiple_of(me * mode_rows + c * rows, rows)

        def shift(i, _, c=c, before=before, mine=mine):
            value = (loc[c, i] + before) * (ngz * depth) ** (-0.5)
            ms_ref[i, pl.ds(mine, rows), :] = value.astype(jnp.bfloat16)
            return 0

        lax.fori_loop(0, depth, shift, 0, unroll=8)
        for d in range(1, nq):
            gather(c, d).start()
        gather_sib(c).start()

    for c in range(chunks):
        for d in range(1, nq):
            gather(c, d).wait_recv()
            forward(c, d).start()
    for c in range(chunks):
        gather_sib(c).wait()
        halo_wait_send(*halo_of(c))
        for d in range(1, nq):
            gather(c, d).wait_send()
            forward(c, d).wait()
        for d in range(1, ngz):
            total(c, d).wait_send()
        for g in range(groups):
            l1(c, g).wait_send()
            for d in range(1, nq):
                l2(c, g, d).wait_send()
    halo_wait_send(*open_args)


def synthesize(weight_ref, shift_ref, pot_ref, out_ref, turned_ref, wide_ref):
    for z in range(shift_ref.shape[0]):
        turned_ref[:, z, :] = pot_ref[z]
        wide_ref[:, z, :] = jnp.dot(
            weight_ref[...], shift_ref[z], preferred_element_type=jnp.float32
        )
    step = 16

    def narrow(i, _):
        at = pl.ds(i * step, step)
        out_ref[at] = (wide_ref[at] * MODES ** (-0.5)).astype(jnp.bfloat16)
        return 0

    lax.fori_loop(0, wide_ref.shape[0] // step, narrow, 0)


def on_device(charge, orders, electrode):
    phi_rows, depth, cells = charge.shape
    n, ngz = lax.axis_size("phi"), lax.axis_size("gz")
    nq = n // 2
    mode_rows = MODES // n
    rows = 16 if mode_rows % 16 == 0 else mode_rows
    chunks = mode_rows // rows
    groups, part = 4, 16
    me = lax.axis_index("phi")
    core = me % 2

    positions = me * phi_rows + jnp.arange(phi_rows, dtype=jnp.int32)
    phase_int = orders[:, None] * positions[None, :] % PHI
    angles = phase_int.astype(jnp.float32) * (2.0 * math.pi / PHI)
    table = jnp.concatenate([jnp.cos(angles), jnp.sin(angles)], 0).astype(jnp.bfloat16)
    blocks = table.reshape(nq, 2, chunks, rows, phi_rows)
    swapped = jnp.where(core == 0, blocks[:, ::-1], blocks)
    basis = swapped.transpose(1, 2, 0, 3, 4).reshape(MODES, phi_rows)

    twice = jnp.concatenate([orders, orders])
    values = lax.dynamic_slice_in_dim(twice, me * mode_rows, mode_rows).astype(jnp.float32)
    cell = jnp.arange(cells, dtype=jnp.int32)
    radius = cell.astype(jnp.float32) + (cells // 2 + 0.5)
    inv = 1.0 / (4.0 + (values[:, None] / radius[None, :]) ** 2)
    inv = inv.reshape(chunks, rows, cells)
    not_last = (cell < cells - 1).astype(jnp.float32)
    not_first = (cell > 0).astype(jnp.float32)
    coef = jnp.stack(
        [
            (1.0 + 0.5 / radius) * not_last,
            (1.0 - 0.5 / radius) * not_first,
            0.5 * not_last,
            0.5 * not_first,
        ]
    )
    coef = jnp.broadcast_to(coef[:, None], (4, 8, cells))
    open_cells = (1 - electrode).astype(jnp.float32)
    open_cells = jnp.broadcast_to(open_cells[:, None], (depth, 8, cells))

    f32, bf16 = jnp.float32, jnp.bfloat16
    wide = depth + 2 * SWEEPS
    sem = pltpu.SemaphoreType.DMA
    vmem = pl.BlockSpec(memory_space=pltpu.VMEM)
    others = nq - 1
    potential, shifts = pl.pallas_call(
        functools.partial(kernel, n, ngz, chunks, groups),
        out_shape=(
            jax.ShapeDtypeStruct((depth, mode_rows, cells), f32),
            jax.ShapeDtypeStruct((depth, MODES, cells), bf16),
        ),
        in_specs=[vmem, pl.BlockSpec(memory_space=pl.ANY)] + [vmem] * 3,
        out_specs=(vmem, vmem),
        scratch_shapes=[
            pltpu.VMEM((depth // part, phi_rows, part, cells), bf16),
            pltpu.VMEM((phi_rows, part, cells), f32),
            sem((depth // part,)),
            pltpu.VMEM((chunks, nq, depth, rows, cells), f32),
            pltpu.VMEM((chunks, nq, depth, rows, cells), f32),
            pltpu.VMEM((chunks, nq, depth, rows, cells), f32),
            pltpu.VMEM((chunks, others, depth, rows, cells), bf16),
            pltpu.VMEM((chunks, others, depth, rows, cells), bf16),
            pltpu.VMEM((wide, 8, cells), f32),
            pltpu.VMEM((chunks, wide, rows, cells), f32),
            pltpu.VMEM((wide, rows, cells), f32),
            pltpu.VMEM((wide, rows, cells), f32),
            pltpu.VMEM((wide, rows, cells), f32),
            pltpu.VMEM((chunks, depth, rows, cells), f32),
            pltpu.VMEM((chunks, rows, cells), f32),
            pltpu.VMEM((chunks, ngz - 1, rows, cells), f32),
            sem((chunks, groups)), sem((chunks, groups)),
            sem((chunks, groups, others)), sem((chunks, groups, others)),
            sem((2,)), sem((2,)),
            sem((chunks, 2)), sem((chunks, 2)),
            sem((chunks, ngz - 1)), sem((chunks, ngz - 1)),
            sem((chunks, others)), sem((chunks, others)),
            sem((chunks,)), sem((chunks,)),
            sem((chunks, others)), sem((chunks, others)),
        ],
        compiler_params=pltpu.CompilerParams(
            collective_id=0, has_side_effects=True, vmem_limit_bytes=48 * 1024 * 1024
        ),
    )(basis, charge, open_cells, inv, coef)

    distortion, potential = pl.pallas_call(
        synthesize,
        grid=(depth // part,),
        out_shape=(
            jax.ShapeDtypeStruct((phi_rows, depth, cells), bf16),
            jax.ShapeDtypeStruct((mode_rows, depth, cells), f32),
        ),
        in_specs=[
            pl.BlockSpec((phi_rows, MODES), lambda i: (0, 0)),
            pl.BlockSpec((part, MODES, cells), lambda i: (i, 0, 0)),
            pl.BlockSpec((part, mode_rows, cells), lambda i: (i, 0, 0)),
        ],
        out_specs=(
            pl.BlockSpec((phi_rows, part, cells), lambda i: (0, i, 0)),
            pl.BlockSpec((mode_rows, part, cells), lambda i: (0, i, 0)),
        ),
        scratch_shapes=[pltpu.VMEM((phi_rows, part, cells), f32)],
        compiler_params=pltpu.CompilerParams(vmem_limit_bytes=32 * 1024 * 1024),
    )(table.T, shifts, potential)
    return (distortion, potential)


def solution(mesh):
    return jax.shard_map(
        on_device,
        mesh=mesh,
        in_specs=(P(("grp", "phi"), "gz", None), P(), P("gz", None)),
        out_specs=(P(("grp", "phi"), "gz", None), P(("grp", "phi"), "gz", None)),
        check_vma=False,
    )
```
